128 devices in a mesh: tm: 8 (over y, core), chan: 16 (over z, x).
Axes of the slice: x: 4, y: 4, z: 4, core: 2. Of those that a mesh axis runs over, the one named last changes fastest.
Arguments:
- samples: float32 [1024, 524288], P('chan', 'tm'), may hold values from -6 to 6
- taps: float32 [1024, 32], P('chan'), may hold values from -1 to 1
- bins: int32 [16], replicated, may hold values from 1 to 127
Outputs:
- csm: float32 [2, 16, 1024, 1024], P(None, None, 'chan', 'tm')
The draws below stay inside these ranges and needn't reach their ends.
Inputs may be any that keep to these rules, and one draw needn't show every extreme that they name: `bins`: bin numbers of the 256-point transform, repeats possible.
All inputs are finite; a program needn't handle non-finite values.
Results may differ from the reference program's by a relative error of at most 0.0013.
Values may be sent and summed in bfloat16 or wider, within the bound.
No kernel may reach another device: no remote copies, remote signals or barrier semaphores. Data moves between devices by JAX's collectives and lax.ppermute only.
A program may use at most 192 MiB of HBM per device.

```python
import jax
import jax.numpy as jnp
from jax import lax

CH_DEV = 64
SEG = 256
NBIN = 16
NTAP = 32
C = 1024
TOTAL = 524288
NSEG_TOT = 4096
N_CHAN = 16


def plant(entries, key, least, largest):
    dims = entries.shape
    spot = [jax.random.randint(jax.random.fold_in(key, axis), (), 0, dims[axis]) for axis in range(len(dims))]
    entries = entries.at[tuple(spot)].set(least)
    longest = dims.index(max(dims))
    spot[longest] = (spot[longest] + 1) % dims[longest]
    return entries.at[tuple(spot)].set(largest)


def block_scale(own_key, extent, shards, least, largest):
    loudness = 1.0
    for axis_at, blocks in shards:
        draws = jax.random.uniform(jax.random.fold_in(jax.random.fold_in(own_key, 6), axis_at), (blocks,), jnp.float32, least / len(shards), largest / len(shards))
        loudness = loudness * jnp.repeat(jnp.exp(draws), extent[axis_at] // blocks).reshape((-1,) + (1,) * (len(extent) - 1 - axis_at))
    return loudness


def noise(own_key, dims, width, most, split=(), kind=jnp.bfloat16):
    drawn = width * jax.random.normal(own_key, dims, jnp.float32)
    if split:
        drawn = drawn * block_scale(own_key, dims, split, -0.22, 0.18)
    return jnp.clip(drawn, -most, most).astype(kind)


def setup_inputs(seed: int = 0) -> dict:
    key_of = jax.random.split(jax.random.key(seed), 4)
    samples = noise(key_of[0], (C, TOTAL), 1.0, 6.0, ((0, 16), (1, 8)), jnp.float32)
    taps = noise(key_of[1], (C, NTAP), NTAP ** -0.5, 1.0, ((0, 16),), jnp.float32)
    bins = plant(jax.random.randint(key_of[2], (NBIN,), 1, SEG // 2), jax.random.fold_in(key_of[2], 1), 1, (SEG // 2) - 1).astype(jnp.int32)
    return {"samples": samples, "taps": taps, "bins": bins}


def make_basis(bins):
    index = jnp.arange(SEG, dtype=jnp.int32)
    window = 0.5 - 0.5 * jnp.cos(2.0 * jnp.pi * index.astype(jnp.float32) / SEG)
    phase_int = (index[:, None] * bins[None, :].astype(jnp.int32)) % SEG
    phase = 2.0 * jnp.pi * phase_int.astype(jnp.float32) / SEG
    return jnp.stack([window[:, None] * jnp.cos(phase), -window[:, None] * jnp.sin(phase)], axis=2)


def equalize(extended, tap_cols, out_len):
    ntap = tap_cols.shape[0]
    total = jnp.zeros((out_len, extended.shape[1]), jnp.float32)
    for k in range(ntap):
        total = total + tap_cols[k][None, :] * extended[ntap - 1 - k:ntap - 1 - k + out_len]
    return total


def reference(samples, taps, bins):
    basis = make_basis(bins)
    hop = SEG // 2
    total_len = samples.shape[1]
    blocks_x = samples.reshape(N_CHAN, CH_DEV, total_len)
    blocks_t = taps.reshape(N_CHAN, CH_DEV, NTAP)

    def one_block(pair):
        xblock, tblock = pair
        extended = jnp.concatenate([jnp.zeros((NTAP - 1, CH_DEV), jnp.float32), xblock.T], axis=0)
        filtered = equalize(extended, tblock.T, total_len)
        framed = jnp.concatenate([jnp.zeros((hop, CH_DEV), jnp.float32), filtered], axis=0)
        pieces = framed.reshape(total_len // hop + 1, hop, CH_DEV)
        spec = jnp.einsum('jhc,hbp->bpcj', pieces[:-1], basis[:hop], precision=lax.Precision.HIGHEST)
        spec = spec + jnp.einsum('jhc,hbp->bpcj', pieces[1:], basis[hop:], precision=lax.Precision.HIGHEST)
        return spec.astype(jnp.bfloat16)

    spectra = lax.map(one_block, (blocks_x, blocks_t))
    spectra = spectra.transpose(1, 2, 0, 3, 4).reshape(NBIN, 2, C, NSEG_TOT)
    scale = 1.0 / (NSEG_TOT * 3.0 * SEG / 8.0)

    def one_bin(spec):
        wide = spec.astype(jnp.float32)
        prod = jnp.einsum('pis,qjs->pqij', wide, wide, precision=lax.Precision.HIGHEST)
        real_part = prod[0, 0] + prod[1, 1]
        imag_part = prod[1, 0] - prod[0, 1]
        return jnp.stack([real_part, imag_part], axis=0) * scale

    csm = lax.map(one_bin, spectra)
    return csm.transpose(1, 0, 2, 3)
```

```python
import functools

import jax
import jax.numpy as jnp
from jax import lax
from jax.experimental import pallas as pl
from jax.experimental.pallas import tpu as pltpu
from jax.sharding import PartitionSpec as P

SEG = 256
HOP = 128
NT = (((1,), (1,)), ((), ()))


def passed_along(block, axis, distance):
    devices = range(lax.axis_size(axis))
    route = [(i - distance, i) for i in devices if i - distance in devices]
    return lax.ppermute(block, axis, route)


def make_basis_rows(bins):
    index = jnp.arange(SEG, dtype=jnp.int32)
    window = 0.5 - 0.5 * jnp.cos(2.0 * jnp.pi * index.astype(jnp.float32) / SEG)
    phase_int = bins[:, None] * index[None, :] % SEG
    phase = 2.0 * jnp.pi * phase_int.astype(jnp.float32) / SEG
    rows = jnp.stack([window * jnp.cos(phase), -window * jnp.sin(phase)], axis=1)
    return rows.reshape(2 * bins.shape[0], SEG)


def tap_basis(taps, bins):
    ntap = taps.shape[1]
    rows = make_basis_rows(bins)
    ext = jnp.pad(rows, ((0, 0), (HOP, ntap - 1)))
    shifted = jnp.stack([ext[:, k : k + 3 * HOP] for k in range(ntap)])
    return jnp.einsum("ck,krq->crq", taps, shifted, precision=lax.Precision.HIGHEST)


def split(value):
    high = value.astype(jnp.bfloat16)
    return high, (value - high.astype(jnp.float32)).astype(jnp.bfloat16)


def spectra_kernel(x_ref, h_ref, v_ref, o_ref, s_ref):
    nrow = o_ref.shape[0]
    nseg = o_ref.shape[2]
    lane = lax.broadcasted_iota(jnp.int32, (nrow, nseg), 1)
    for c in range(16):
        g, r = divmod(c, 8)
        x = x_ref[g, pl.ds(r, nseg, stride=8), :]
        data = jnp.concatenate(split(x), axis=1)
        v = v_ref[c]
        vh, vl = split(v)
        high = jnp.concatenate([vh[:, i * HOP : (i + 1) * HOP] for i in range(3)], axis=0)
        low = jnp.concatenate([vl[:, i * HOP : (i + 1) * HOP] for i in range(3)], axis=0)
        weights = jnp.concatenate(
            [
                jnp.concatenate([high, high], axis=1),
                jnp.concatenate([low, jnp.zeros_like(low)], axis=1),
            ],
            axis=0,
        )
        z = lax.dot_general(weights, data, NT, preferred_element_type=jnp.float32)
        z = z[: 3 * nrow] + z[3 * nrow :]
        older = h_ref[g, r : r + 1, :]
        newer = h_ref[g, 8 + r : 9 + r, :]
        first = jnp.sum(v[:, HOP : 2 * HOP] * newer + v[:, :HOP] * older, axis=1, keepdims=True)
        second = jnp.sum(v[:, :HOP] * newer, axis=1, keepdims=True)
        z1 = jnp.where(lane == 0, first, pltpu.roll(z[nrow : 2 * nrow], 1, 1))
        z0 = jnp.where(lane == 1, second, pltpu.roll(z[:nrow], 2, 1))
        z0 = jnp.where(lane == 0, 0.0, z0)
        total = z[2 * nrow :] + z1 + z0
        for i in range(nseg // 128):
            s_ref[i, pl.ds(c, nrow, stride=16), :] = total[:, i * 128 : (i + 1) * 128]
    for j in range(nrow):
        for i in range(nseg // 128):
            part = s_ref[i, j * 16 : (j + 1) * 16, :]
            o_ref[j, :, i * 128 : (i + 1) * 128] = part.astype(jnp.bfloat16)


def spectra(samples, before, weights):
    width, span = samples.shape
    nseg = span // HOP
    nrow = weights.shape[1]

    def by_rows(a):
        n = a.shape[1] // HOP
        return a.reshape(width // 8, 8, n, HOP).transpose(0, 2, 1, 3).reshape(width // 8, n * 8, HOP)

    return pl.pallas_call(
        spectra_kernel,
        grid=(width // 16,),
        in_specs=[
            pl.BlockSpec((2, nseg * 8, HOP), lambda i: (i, 0, 0)),
            pl.BlockSpec((2, 16, HOP), lambda i: (i, 0, 0)),
            pl.BlockSpec((16, nrow, 3 * HOP), lambda i: (i, 0, 0)),
        ],
        out_specs=pl.BlockSpec((nrow, 16, nseg), lambda i: (0, i, 0)),
        out_shape=jax.ShapeDtypeStruct((nrow, width, nseg), jnp.bfloat16),
        scratch_shapes=[pltpu.VMEM((nseg // 128, nrow * 16, 128), jnp.float32)],
        compiler_params=pltpu.CompilerParams(vmem_limit_bytes=48 * 2**20),
        cost_estimate=pl.CostEstimate(
            flops=2 * 2 * 6 * nrow * width * span, bytes_accessed=width * span * 4, transcendentals=0
        ),
        name="spectra",
    )(by_rows(samples), by_rows(before), weights)


def csm_kernel(scale, x_ref, o_ref):
    nsrc, _, width, nseg = x_ref.shape
    take = 256 // width
    j = pl.program_id(0)
    real = x_ref[:, 0].reshape(nsrc * width, nseg)
    imag = x_ref[:, 1].reshape(nsrc * width, nseg)
    cols = x_ref[pl.ds(j * take, take)]
    creal = cols[:, 0].reshape(256, nseg)
    cimag = cols[:, 1].reshape(256, nseg)

    def dot(a, b):
        return lax.dot_general(a, b, NT, preferred_element_type=jnp.float32)

    re = (dot(real, creal) + dot(imag, cimag)) * scale
    for i in range(2):
        o_ref[i, :, 0] = re[:, i * 128 : (i + 1) * 128].reshape(nsrc, width, 128)
    im = (dot(imag, creal) - dot(real, cimag)) * scale
    for i in range(2):
        o_ref[i, :, 1] = im[:, i * 128 : (i + 1) * 128].reshape(nsrc, width, 128)


def csm_partial(x, scale):
    nsrc, _, width, nseg = x.shape
    chans = nsrc * width
    return pl.pallas_call(
        functools.partial(csm_kernel, scale),
        grid=(chans // 256,),
        in_specs=[pl.BlockSpec(x.shape, lambda j: (0, 0, 0, 0))],
        out_specs=pl.BlockSpec((2, nsrc, 2, width, 128), lambda j: (j, 0, 0, 0, 0)),
        out_shape=jax.ShapeDtypeStruct((chans // 128, nsrc, 2, width, 128), jnp.float32),
        compiler_params=pltpu.CompilerParams(vmem_limit_bytes=48 * 2**20),
        cost_estimate=pl.CostEstimate(
            flops=8 * chans * chans * nseg, bytes_accessed=chans * chans * 8, transcendentals=0
        ),
        name="csm",
    )(x)


def body(samples, taps, bins):
    width, span = samples.shape
    nbin = bins.shape[0]
    before = passed_along(samples[:, span - SEG :], "tm", 1)
    own = spectra(samples, before, tap_basis(taps, bins))
    own = own.reshape(nbin, 2, width, span // HOP)
    mine = lax.all_to_all(own, "chan", 0, 0)
    segments_all = lax.axis_size("tm") * (span // HOP)
    partial = csm_partial(mine, 1.0 / (segments_all * 3.0 * SEG / 8.0))
    summed = lax.psum_scatter(partial, "tm", scatter_dimension=0)
    rows = lax.all_to_all(summed, "chan", 0, 0)
    return rows.transpose(1, 0, 2, 3)


def solution(mesh):
    return jax.shard_map(
        body,
        mesh=mesh,
        in_specs=(P("chan", "tm"), P("chan", None), P()),
        out_specs=P(None, None, "chan", "tm"),
        check_vma=False,
    )
```

```python
import functools

import jax
import jax.numpy as jnp
from jax import lax
from jax.experimental import pallas as pl
from jax.experimental.pallas import tpu as pltpu
from jax.sharding import PartitionSpec as P

SEG = 256
HOP = 128
CODE = 32700.0
LEVELS = 64.0
NT = (((1,), (1,)), ((), ()))


def passed_along(block, axis, distance):
    devices = range(lax.axis_size(axis))
    route = [(i - distance, i) for i in devices if i - distance in devices]
    return lax.ppermute(block, axis, route)


def make_basis_rows(bins):
    index = jnp.arange(SEG, dtype=jnp.int32)
    window = 0.5 - 0.5 * jnp.cos(2.0 * jnp.pi * index.astype(jnp.float32) / SEG)
    phase_int = bins[:, None] * index[None, :] % SEG
    phase = 2.0 * jnp.pi * phase_int.astype(jnp.float32) / SEG
    rows = jnp.stack([window * jnp.cos(phase), -window * jnp.sin(phase)], axis=1)
    return rows.reshape(2 * bins.shape[0], SEG)


def weights_kernel(t_ref, b_ref, o_ref):
    nrow = b_ref.shape[0]
    width, ntap = t_ref.shape
    size = b_ref.shape[1]
    th, tl = split(t_ref[...])
    lhs = jnp.concatenate([th, tl, th], axis=1)
    for row in range(nrow):
        line = jnp.broadcast_to(b_ref[row : row + 1, :], (ntap, size))
        line = pltpu.roll(line, size - ntap + 1, 1, stride=1, stride_axis=0)
        high, low = split(line[:, : 3 * HOP])
        rhs = jnp.concatenate([high, high, low], axis=0)
        out = jnp.dot(lhs, rhs, preferred_element_type=jnp.float32)
        for g in range(3):
            for i in range(width // 8):
                part = out[i * 8 : (i + 1) * 8, g * HOP : (g + 1) * HOP]
                o_ref[g, pl.ds(i * 8 * nrow + row, 8, stride=nrow), :] = part


def tap_basis(taps, bins):
    width, ntap = taps.shape
    nrow = 2 * bins.shape[0]
    ext = jnp.pad(make_basis_rows(bins), ((0, 0), (HOP, HOP)))
    return pl.pallas_call(
        weights_kernel,
        out_shape=jax.ShapeDtypeStruct((3, width * nrow, HOP), jnp.float32),
        compiler_params=pltpu.CompilerParams(vmem_limit_bytes=32 * 2**20),
        cost_estimate=pl.CostEstimate(
            flops=18 * ntap * nrow * width * HOP,
            bytes_accessed=12 * width * nrow * HOP,
            transcendentals=0,
        ),
        name="weights",
    )(taps[:, ::-1], ext)


def split(value):
    high = value.astype(jnp.bfloat16)
    return high, (value - high.astype(jnp.float32)).astype(jnp.bfloat16)


def spectra_kernel(x_ref, h_ref, v_ref, o_ref, s_ref):
    nrow = 2 * o_ref.shape[0]
    nseg = o_ref.shape[2] // 2
    lane = lax.broadcasted_iota(jnp.int32, (nrow, nseg), 1)
    for c in range(16):
        g, r = divmod(c, 8)
        x = x_ref[g, pl.ds(r, nseg, stride=8), :]
        data = jnp.concatenate(split(x), axis=1)
        v = v_ref[:, c * nrow : (c + 1) * nrow, :]
        high, low = split(v.reshape(3 * nrow, HOP))
        weights = jnp.concatenate(
            [
                jnp.concatenate([high, high], axis=1),
                jnp.concatenate([low, jnp.zeros_like(low)], axis=1),
            ],
            axis=0,
        )
        z = lax.dot_general(weights, data, NT, preferred_element_type=jnp.float32)
        z = z[: 3 * nrow] + z[3 * nrow :]
        older = h_ref[g, r : r + 1, :]
        newer = h_ref[g, 8 + r : 9 + r, :]
        first = jnp.sum(v[1] * newer + v[0] * older, axis=1, keepdims=True)
        second = jnp.sum(v[0] * newer, axis=1, keepdims=True)
        z1 = jnp.where(lane == 0, first, pltpu.roll(z[nrow : 2 * nrow], 1, 1))
        z0 = jnp.where(lane == 1, second, pltpu.roll(z[:nrow], 2, 1))
        z0 = jnp.where(lane == 0, 0.0, z0)
        total = z[2 * nrow :] + z1 + z0
        for i in range(nseg // 128):
            s_ref[i, pl.ds(c, nrow, stride=16), :] = total[:, i * 128 : (i + 1) * 128]
    for j in range(nrow):
        for i in range(nseg // 128):
            part = s_ref[i, j * 16 : (j + 1) * 16, :]
            at = j % 2 * nseg + i * 128
            o_ref[j // 2, :, at : at + 128] = part.astype(jnp.bfloat16)


def spectra(samples, before, weights):
    width, span = samples.shape
    nseg = span // HOP
    nrow = weights.shape[1] // width

    def by_rows(a):
        n = a.shape[1] // HOP
        return a.reshape(width // 8, 8, n, HOP).transpose(0, 2, 1, 3).reshape(width // 8, n * 8, HOP)

    return pl.pallas_call(
        spectra_kernel,
        grid=(width // 16,),
        in_specs=[
            pl.BlockSpec((2, nseg * 8, HOP), lambda i: (i, 0, 0)),
            pl.BlockSpec((2, 16, HOP), lambda i: (i, 0, 0)),
            pl.BlockSpec((3, 16 * nrow, HOP), lambda i: (0, i, 0)),
        ],
        out_specs=pl.BlockSpec((nrow // 2, 16, 2 * nseg), lambda i: (0, i, 0)),
        out_shape=jax.ShapeDtypeStruct((nrow // 2, width, 2 * nseg), jnp.bfloat16),
        scratch_shapes=[pltpu.VMEM((nseg // 128, nrow * 16, 128), jnp.float32)],
        compiler_params=pltpu.CompilerParams(vmem_limit_bytes=48 * 2**20),
        cost_estimate=pl.CostEstimate(
            flops=2 * 2 * 6 * nrow * width * span, bytes_accessed=width * span * 4, transcendentals=0
        ),
        name="spectra",
    )(by_rows(samples), by_rows(before), weights)


def csm_kernel(core_ref, own_ref, other_ref, o_ref, p_ref):
    nsrc, width, depth = own_ref.shape
    nseg = depth // 2
    blocks = o_ref.shape[0]
    chans = nsrc * width
    take = HOP // width
    core = core_ref[0]
    largest = jnp.zeros((1, 2 * HOP), jnp.float32)
    for y in range(blocks):
        at = (2 * y + core) * take

        def columns(ref):
            cols = ref[pl.ds(at, take)].reshape(HOP, depth)
            turned = jnp.concatenate([-cols[:, nseg:], cols[:, :nseg]], axis=1)
            return jnp.concatenate([cols, turned], axis=0)

        own, other = columns(own_ref), columns(other_ref)
        for r in range(0, nsrc, 4):
            rows = pl.ds(r * width, 4 * width)
            part = lax.dot_general(
                own_ref[r : r + 4].reshape(4 * width, depth),
                own,
                NT,
                preferred_element_type=jnp.float32,
            ) + lax.dot_general(
                other_ref[r : r + 4].reshape(4 * width, depth),
                other,
                NT,
                preferred_element_type=jnp.float32,
            )
            p_ref[y, rows, :] = part
            largest = jnp.maximum(largest, jnp.max(jnp.abs(part), axis=0, keepdims=True))
    top = jnp.max(largest, axis=1, keepdims=True)
    level = jnp.ceil(jnp.log2(jnp.maximum(top, 1e-30)) * LEVELS)
    gain = CODE * CODE * jnp.exp2(level * (-1.0 / LEVELS))
    mark = jnp.broadcast_to(level, (16, HOP)).astype(jnp.int32).astype(jnp.int16)
    for y in range(blocks):
        for r in range(nsrc):
            part = p_ref[y, r * width : (r + 1) * width, :]
            code = (jnp.sqrt(jnp.abs(part) * gain) + 0.5).astype(jnp.int32)
            code = jnp.where(part < 0.0, -code, code).astype(jnp.int16)
            o_ref[y, r, :width] = code[:, :HOP]
            o_ref[y, r, width : 2 * width] = code[:, HOP:]
            o_ref[y, r, 2 * width :] = mark


def csm_codes(core, own, other, blocks):
    nsrc, width, depth = own.shape
    chans = nsrc * width
    return pl.pallas_call(
        csm_kernel,
        in_specs=[
            pl.BlockSpec(memory_space=pltpu.SMEM),
            pl.BlockSpec(memory_space=pltpu.VMEM),
            pl.BlockSpec(memory_space=pltpu.VMEM),
        ],
        out_specs=pl.BlockSpec(memory_space=pltpu.VMEM),
        out_shape=jax.ShapeDtypeStruct((blocks, nsrc, 2 * width + 16, HOP), jnp.int16),
        scratch_shapes=[pltpu.VMEM((blocks, chans, 2 * HOP), jnp.float32)],
        compiler_params=pltpu.CompilerParams(vmem_limit_bytes=48 * 2**20),
        cost_estimate=pl.CostEstimate(
            flops=8 * chans * blocks * HOP * depth,
            bytes_accessed=4 * chans * (depth + blocks * HOP),
            transcendentals=0,
        ),
        name="csm",
    )(core, own, other)


def total_kernel(scale, c_ref, o_ref):
    blocks, nbin, _, _ = c_ref.shape
    width = o_ref.shape[2]
    for b in range(nbin):
        total = jnp.zeros((2 * width, HOP), jnp.float32)
        for y in range(blocks):
            mark = c_ref[y, b, 2 * width :].astype(jnp.int32).astype(jnp.float32)
            step = jnp.exp2(mark * (1.0 / LEVELS))[:1] * (scale / (CODE * CODE))
            code = c_ref[y, b, : 2 * width].astype(jnp.int32).astype(jnp.float32)
            total = total + code * jnp.abs(code) * step
        o_ref[0, b] = total[:width]
        o_ref[1, b] = total[width:]


def total_of(codes, scale):
    blocks, nbin, height, _ = codes.shape
    width = (height - 16) // 2
    return pl.pallas_call(
        functools.partial(total_kernel, scale),
        grid=(nbin // 4,),
        in_specs=[pl.BlockSpec((blocks, 4, height, HOP), lambda i: (0, i, 0, 0))],
        out_specs=pl.BlockSpec((2, 4, width, HOP), lambda i: (0, i, 0, 0)),
        out_shape=jax.ShapeDtypeStruct((2, nbin, width, HOP), jnp.float32),
        compiler_params=pltpu.CompilerParams(vmem_limit_bytes=32 * 2**20),
        cost_estimate=pl.CostEstimate(
            flops=6 * blocks * nbin * height * HOP,
            bytes_accessed=3 * blocks * nbin * height * HOP,
            transcendentals=0,
        ),
        name="total",
    )(codes)


def body(samples, taps, bins):
    width, span = samples.shape
    times, chans = lax.axis_size("tm"), lax.axis_size("chan")
    before = passed_along(samples[:, span - SEG :], "tm", 1)
    own = spectra(samples, before, tap_basis(taps, bins))
    mine = lax.all_to_all(own, "chan", 0, 0)
    other = lax.ppermute(mine, "tm", [(i, i ^ 1) for i in range(times)])
    core = (lax.axis_index("tm") % 2).astype(jnp.int32).reshape(1)
    codes = csm_codes(core, mine, other, times // 2)
    height = codes.shape[2]
    same_core = [[t * chans + c for t in range(h, times, 2) for c in range(chans)] for h in range(2)]
    codes = lax.all_to_all(
        codes.reshape(times // 2 * chans, height, HOP),
        ("tm", "chan"),
        0,
        0,
        axis_index_groups=same_core,
    )
    scale = 1.0 / (times * (span // HOP) * 3.0 * SEG / 8.0)
    return total_of(codes.reshape(times // 2, chans, height, HOP), scale)


def solution(mesh):
    return jax.shard_map(
        body,
        mesh=mesh,
        in_specs=(P("chan", "tm"), P("chan", None), P()),
        out_specs=P(None, None, "chan", "tm"),
        check_vma=False,
    )
```

```python
import functools
import math

import jax
import jax.numpy as jnp
from jax import lax
from jax.experimental import pallas as pl
from jax.experimental.pallas import tpu as pltpu
from jax.sharding import PartitionSpec as P

SEG = 256
HOP = 128
LEAST = 2.0**-64
STEPS = 312.0
NT = (((1,), (1,)), ((), ()))


def passed_along(block, axis, distance):
    devices = range(lax.axis_size(axis))
    route = [(i - distance, i) for i in devices if i - distance in devices]
    return lax.ppermute(block, axis, route)


def weights_kernel(bins_ref, t_ref, o_ref, b_ref):
    nbin = bins_ref.shape[1]
    nrow, size = b_ref.shape
    ntap, width = t_ref.shape
    index = lax.broadcasted_iota(jnp.int32, (nrow, SEG), 1)
    odd = lax.broadcasted_iota(jnp.int32, (nrow, SEG), 0) % 2
    own_bin = lax.broadcasted_iota(jnp.int32, (nrow, nbin), 0) // 2
    own_bin = own_bin == lax.broadcasted_iota(jnp.int32, (nrow, nbin), 1)
    bins = jnp.where(own_bin, bins_ref[...].astype(jnp.float32), 0.0)
    bins = jnp.sum(bins, axis=1, keepdims=True).astype(jnp.int32)
    window = 0.5 - 0.5 * jnp.cos(2.0 * jnp.pi * index.astype(jnp.float32) / SEG)
    phase = 2.0 * jnp.pi * ((bins * index) & (SEG - 1)).astype(jnp.float32) / SEG
    wave = jnp.where(odd == 0, jnp.cos(phase), -jnp.sin(phase))
    b_ref[:, :HOP] = jnp.zeros((nrow, HOP), jnp.float32)
    b_ref[:, HOP : HOP + SEG] = window * wave
    b_ref[:, HOP + SEG :] = jnp.zeros((nrow, HOP), jnp.float32)
    turn = lax.broadcasted_iota(jnp.int32, (ntap, ntap), 0)
    turn = turn + lax.broadcasted_iota(jnp.int32, (ntap, ntap), 1) == ntap - 1
    turn = jnp.where(turn, 1.0, 0.0).astype(jnp.bfloat16)
    th, tl = split(t_ref[...].T)
    th = jnp.dot(th, turn, preferred_element_type=jnp.float32).astype(jnp.bfloat16)
    tl = jnp.dot(tl, turn, preferred_element_type=jnp.float32).astype(jnp.bfloat16)
    lhs = jnp.concatenate([th, tl, th], axis=1)
    for row in range(nrow):
        line = jnp.broadcast_to(b_ref[row : row + 1, :], (ntap, size))
        line = pltpu.roll(line, size - ntap + 1, 1, stride=1, stride_axis=0)
        high, low = split(line[:, : 3 * HOP])
        rhs = jnp.concatenate([high, high, low], axis=0)
        out = jnp.dot(lhs, rhs, preferred_element_type=jnp.float32)
        for g in range(3):
            o_ref[g * nrow + row] = out[:, g * HOP : (g + 1) * HOP]


def tap_basis(taps, bins):
    width, ntap = taps.shape
    nrow = 2 * bins.shape[0]
    return pl.pallas_call(
        weights_kernel,
        out_shape=jax.ShapeDtypeStruct((3 * nrow, width, HOP), jnp.float32),
        scratch_shapes=[pltpu.VMEM((nrow, 4 * HOP), jnp.float32)],
        compiler_params=pltpu.CompilerParams(vmem_limit_bytes=32 * 2**20),
        cost_estimate=pl.CostEstimate(
            flops=18 * ntap * nrow * width * HOP,
            bytes_accessed=12 * width * nrow * HOP,
            transcendentals=0,
        ),
        name="weights",
    )(bins.reshape(1, -1), taps.T)


def split(value):
    high = value.astype(jnp.bfloat16)
    return high, (value - high.astype(jnp.float32)).astype(jnp.bfloat16)


def spectra_kernel(x_ref, h_ref, v_ref, o_ref, s_ref):
    nrow = 2 * o_ref.shape[0]
    nseg = o_ref.shape[2] // 2
    lines = v_ref.reshape(3 * nrow * 16, HOP)
    lane = lax.broadcasted_iota(jnp.int32, (nrow, nseg), 1)
    for c in range(16):
        g, r = divmod(c, 8)
        x = x_ref[g, pl.ds(r, nseg, stride=8), :]
        data = jnp.concatenate(split(x), axis=1)
        v = lines[pl.ds(c, 3 * nrow, stride=16), :]
        high, low = split(v)
        weights = jnp.concatenate(
            [
                jnp.concatenate([high, high], axis=1),
                jnp.concatenate([low, jnp.zeros_like(low)], axis=1),
            ],
            axis=0,
        )
        z = lax.dot_general(weights, data, NT, preferred_element_type=jnp.float32)
        z = z[: 3 * nrow] + z[3 * nrow :]
        older = h_ref[g, r : r + 1, :]
        newer = h_ref[g, 8 + r : 9 + r, :]
        first = jnp.sum(v[nrow : 2 * nrow] * newer + v[:nrow] * older, axis=1, keepdims=True)
        second = jnp.sum(v[:nrow] * newer, axis=1, keepdims=True)
        z1 = jnp.where(lane == 0, first, pltpu.roll(z[nrow : 2 * nrow], 1, 1))
        z0 = jnp.where(lane == 1, second, pltpu.roll(z[:nrow], 2, 1))
        z0 = jnp.where(lane == 0, 0.0, z0)
        total = z[2 * nrow :] + z1 + z0
        for i in range(nseg // 128):
            s_ref[i, pl.ds(c, nrow, stride=16), :] = total[:, i * 128 : (i + 1) * 128]
    for j in range(nrow):
        for i in range(nseg // 128):
            part = s_ref[i, j * 16 : (j + 1) * 16, :]
            at = j % 2 * nseg + i * 128
            o_ref[j // 2, :, at : at + 128] = part.astype(jnp.bfloat16)


def spectra(samples, before, weights):
    width, span = samples.shape
    nseg = span // HOP
    nrow = weights.shape[0] // 3

    def by_rows(a):
        n = a.shape[1] // HOP
        return a.reshape(width // 8, 8, n, HOP).transpose(0, 2, 1, 3).reshape(width // 8, n * 8, HOP)

    return pl.pallas_call(
        spectra_kernel,
        grid=(width // 16,),
        in_specs=[
            pl.BlockSpec((2, nseg * 8, HOP), lambda i: (i, 0, 0)),
            pl.BlockSpec((2, 16, HOP), lambda i: (i, 0, 0)),
            pl.BlockSpec((3 * nrow, 16, HOP), lambda i: (0, i, 0)),
        ],
        out_specs=pl.BlockSpec((nrow // 2, 16, 2 * nseg), lambda i: (0, i, 0)),
        out_shape=jax.ShapeDtypeStruct((nrow // 2, width, 2 * nseg), jnp.bfloat16),
        scratch_shapes=[pltpu.VMEM((nseg // 128, nrow * 16, 128), jnp.float32)],
        compiler_params=pltpu.CompilerParams(vmem_limit_bytes=48 * 2**20),
        cost_estimate=pl.CostEstimate(
            flops=2 * 2 * 6 * nrow * width * span, bytes_accessed=width * span * 4, transcendentals=0
        ),
        name="spectra",
    )(by_rows(samples), by_rows(before), weights)


def columns_of(ref, at):
    _, width, depth = ref.shape
    nseg = depth // 2
    cols = ref[pl.ds(at, HOP // width)].reshape(HOP, depth)
    turned = jnp.concatenate([-cols[:, nseg:], cols[:, :nseg]], axis=1)
    return jnp.concatenate([cols, turned], axis=0)


def product(ref, r, columns):
    _, width, depth = ref.shape
    rows = ref[r : r + 4].reshape(4 * width, depth)
    return lax.dot_general(rows, columns, NT, preferred_element_type=jnp.float32)


def own_kernel(core_ref, own_ref, p_ref):
    nsrc, width, _ = own_ref.shape
    core = core_ref[0]
    for y in range(p_ref.shape[0]):
        own = columns_of(own_ref, (2 * y + core) * (HOP // width))
        for r in range(0, nsrc, 4):
            p_ref[y, r * width : (r + 4) * width, :] = product(own_ref, r, own)


def code_kernel(core_ref, other_ref, p_ref, o_ref):
    nsrc, width, _ = other_ref.shape
    core = core_ref[0]
    for y in range(p_ref.shape[0]):
        other = columns_of(other_ref, (2 * y + core) * (HOP // width))
        for r in range(0, nsrc, 4):
            part = product(other_ref, r, other) + p_ref[y, r * width : (r + 4) * width, :]
            level = jnp.log2(jnp.maximum(jnp.abs(part), LEAST))
            code = (level * STEPS + (0.5 - math.log2(LEAST) * STEPS)).astype(jnp.int32)
            code = jnp.where(part < 0.0, -code, code).astype(jnp.int16)
            code = code.reshape(4, width, 2 * HOP)
            o_ref[y, r : r + 4, :width] = code[:, :, :HOP]
            o_ref[y, r : r + 4, width:] = code[:, :, HOP:]


def own_products(core, own, blocks):
    nsrc, width, depth = own.shape
    chans = nsrc * width
    return pl.pallas_call(
        own_kernel,
        in_specs=[
            pl.BlockSpec(memory_space=pltpu.SMEM),
            pl.BlockSpec(memory_space=pltpu.VMEM),
        ],
        out_specs=pl.BlockSpec(memory_space=pltpu.VMEM),
        out_shape=jax.ShapeDtypeStruct((blocks, chans, 2 * HOP), jnp.float32),
        compiler_params=pltpu.CompilerParams(vmem_limit_bytes=24 * 2**20),
        cost_estimate=pl.CostEstimate(
            flops=4 * chans * blocks * HOP * depth,
            bytes_accessed=2 * chans * (depth + 4 * blocks * HOP),
            transcendentals=0,
        ),
        name="own_products",
    )(core, own)


def product_codes(core, other, partial):
    nsrc, width, depth = other.shape
    blocks, chans, _ = partial.shape
    return pl.pallas_call(
        code_kernel,
        in_specs=[
            pl.BlockSpec(memory_space=pltpu.SMEM),
            pl.BlockSpec(memory_space=pltpu.VMEM),
            pl.BlockSpec(memory_space=pltpu.VMEM),
        ],
        out_specs=pl.BlockSpec(memory_space=pltpu.VMEM),
        out_shape=jax.ShapeDtypeStruct((blocks, nsrc, 2 * width, HOP), jnp.int16),
        compiler_params=pltpu.CompilerParams(vmem_limit_bytes=32 * 2**20),
        cost_estimate=pl.CostEstimate(
            flops=4 * chans * blocks * HOP * depth,
            bytes_accessed=2 * chans * (depth + 6 * blocks * HOP),
            transcendentals=chans * blocks * HOP * 2,
        ),
        name="product_codes",
    )(core, other, partial)


def total_kernel(scale, c_ref, o_ref):
    blocks, nbin, _, _ = c_ref.shape
    width = o_ref.shape[2]
    for b in range(nbin):
        total = jnp.zeros((2 * width, HOP), jnp.float32)
        for y in range(blocks):
            code = c_ref[y, b].astype(jnp.int32).astype(jnp.float32)
            level = jnp.abs(code) * (1.0 / STEPS) + math.log2(LEAST * scale)
            size = jnp.exp2(level)
            total = total + jnp.where(code > 0.0, size, jnp.where(code < 0.0, -size, 0.0))
        o_ref[0, b] = total[:width]
        o_ref[1, b] = total[width:]


def total_of(codes, scale):
    blocks, nbin, height, _ = codes.shape
    width = height // 2
    return pl.pallas_call(
        functools.partial(total_kernel, scale),
        grid=(nbin // 4,),
        in_specs=[pl.BlockSpec((blocks, 4, height, HOP), lambda i: (0, i, 0, 0))],
        out_specs=pl.BlockSpec((2, 4, width, HOP), lambda i: (0, i, 0, 0)),
        out_shape=jax.ShapeDtypeStruct((2, nbin, width, HOP), jnp.float32),
        compiler_params=pltpu.CompilerParams(vmem_limit_bytes=32 * 2**20),
        cost_estimate=pl.CostEstimate(
            flops=6 * blocks * nbin * height * HOP,
            bytes_accessed=3 * blocks * nbin * height * HOP,
            transcendentals=blocks * nbin * height * HOP,
        ),
        name="total",
    )(codes)


def body(samples, taps, bins):
    width, span = samples.shape
    times, chans = lax.axis_size("tm"), lax.axis_size("chan")
    before = passed_along(samples[:, span - SEG :], "tm", 1)
    own = spectra(samples, before, tap_basis(taps, bins))
    mine = lax.all_to_all(own, "chan", 0, 0)
    other = lax.ppermute(mine, "tm", [(i, i ^ 1) for i in range(times)])
    core = (lax.axis_index("tm") % 2).astype(jnp.int32).reshape(1)
    codes = product_codes(core, other, own_products(core, mine, times // 2))
    height = codes.shape[2]
    same_core = [[t * chans + c for t in range(h, times, 2) for c in range(chans)] for h in range(2)]
    codes = lax.all_to_all(
        codes.reshape(times // 2 * chans, height, HOP),
        ("tm", "chan"),
        0,
        0,
        axis_index_groups=same_core,
    )
    scale = 1.0 / (times * (span // HOP) * 3.0 * SEG / 8.0)
    return total_of(codes.reshape(times // 2, chans, height, HOP), scale)


def solution(mesh):
    return jax.shard_map(
        body,
        mesh=mesh,
        in_specs=(P("chan", "tm"), P("chan", None), P()),
        out_specs=P(None, None, "chan", "tm"),
        check_vma=False,
    )
```

```python
import functools
import math

import jax
import jax.numpy as jnp
from jax import lax
from jax.experimental import pallas as pl
from jax.experimental.pallas import tpu as pltpu
from jax.sharding import PartitionSpec as P

SEG = 256
HOP = 128
LEAST = 2.0**-64
STEPS = 312.0
NT = (((1,), (1,)), ((), ()))


def passed_along(block, axis, distance):
    devices = range(lax.axis_size(axis))
    route = [(i - distance, i) for i in devices if i - distance in devices]
    return lax.ppermute(block, axis, route)


def split(value):
    high = value.astype(jnp.bfloat16)
    return high, (value - high.astype(jnp.float32)).astype(jnp.bfloat16)


def fill_weights(t_ref, b_ref, v_ref):
    nrow, size = b_ref.shape
    nbin = nrow // 2
    ntap, width = t_ref.shape[0] - 8, t_ref.shape[1]
    index = lax.broadcasted_iota(jnp.int32, (nrow, SEG), 1)
    odd = lax.broadcasted_iota(jnp.int32, (nrow, SEG), 0) % 2
    own_bin = lax.broadcasted_iota(jnp.int32, (nrow, nbin), 0) // 2
    own_bin = own_bin == lax.broadcasted_iota(jnp.int32, (nrow, nbin), 1)
    bins = jnp.where(own_bin, t_ref[ntap : ntap + 1, :nbin], 0.0)
    bins = jnp.sum(bins, axis=1, keepdims=True).astype(jnp.int32)
    window = 0.5 - 0.5 * jnp.cos(2.0 * jnp.pi * index.astype(jnp.float32) / SEG)
    phase = 2.0 * jnp.pi * ((bins * index) & (SEG - 1)).astype(jnp.float32) / SEG
    wave = jnp.where(odd == 0, jnp.cos(phase), -jnp.sin(phase))
    b_ref[:, :HOP] = jnp.zeros((nrow, HOP), jnp.float32)
    b_ref[:, HOP : HOP + SEG] = window * wave
    b_ref[:, HOP + SEG :] = jnp.zeros((nrow, HOP), jnp.float32)
    turn = lax.broadcasted_iota(jnp.int32, (ntap, ntap), 0)
    turn = turn + lax.broadcasted_iota(jnp.int32, (ntap, ntap), 1) == ntap - 1
    turn = jnp.where(turn, 1.0, 0.0).astype(jnp.bfloat16)
    th, tl = split(t_ref[:ntap].T)
    th = jnp.dot(th, turn, preferred_element_type=jnp.float32).astype(jnp.bfloat16)
    tl = jnp.dot(tl, turn, preferred_element_type=jnp.float32).astype(jnp.bfloat16)
    lhs = jnp.concatenate([th, tl, th], axis=1)
    for row in range(nrow):
        line = jnp.broadcast_to(b_ref[row : row + 1, :], (ntap, size))
        line = pltpu.roll(line, size - ntap + 1, 1, stride=1, stride_axis=0)
        high, low = split(line[:, : 3 * HOP])
        rhs = jnp.concatenate([high, high, low], axis=0)
        out = jnp.dot(lhs, rhs, preferred_element_type=jnp.float32)
        for g in range(3):
            for i in range(width // 16):
                at = ((i * 3 + g) * nrow + row) * 16
                part = out[i * 16 : (i + 1) * 16, g * HOP : (g + 1) * HOP]
                v_ref[at : at + 16, :] = part


def taps_and_bins(taps, bins):
    width, ntap = taps.shape
    below = lax.broadcasted_iota(jnp.int32, (ntap + 8, width), 0) >= ntap
    bins = jnp.pad(bins.astype(jnp.float32), (0, width - bins.shape[0]))
    return jnp.where(below, bins[None, :], jnp.pad(taps.T, ((0, 8), (0, 0))))


def spectra_kernel(t_ref, x_ref, h_ref, o_ref, b_ref, v_ref, x_buf, s_ref, sems):
    nrow = 2 * o_ref.shape[0]
    width = o_ref.shape[1]
    nseg = o_ref.shape[2] // 2
    groups = width // 8
    copies = [
        pltpu.make_async_copy(x_ref.at[g], x_buf.at[g], sems.at[g]) for g in range(groups)
    ]
    waits = {0: copies[:1], 1: copies[1:2], 2: copies[2:4], 4: copies[4:]}
    starts = {1: copies[4:6], 2: copies[6:]}
    for copy in copies[:4]:
        copy.start()
    fill_weights(t_ref, b_ref, v_ref)
    lane = lax.broadcasted_iota(jnp.int32, (nrow, HOP), 1)

    def finish(i, j):
        for k in range(nseg // 128):
            part = s_ref[i % 2, k, j * 16 : (j + 1) * 16, :]
            at = j % 2 * nseg + k * 128
            o_ref[j // 2, i * 16 : (i + 1) * 16, at : at + 128] = part.astype(jnp.bfloat16)

    for c in range(width):
        g, r = divmod(c, 8)
        i, c16 = divmod(c, 16)
        if r == 0:
            for copy in waits.get(g, []):
                copy.wait()
            for copy in starts.get(g, []):
                copy.start()
        x = x_buf[g, pl.ds(r, nseg, stride=8), :]
        data = jnp.concatenate(split(x), axis=1)
        v = v_ref[pl.ds(i * 3 * nrow * 16 + c16, 3 * nrow, stride=16), :]
        high, low = split(v)
        weights = jnp.concatenate(
            [
                jnp.concatenate([high, high], axis=1),
                jnp.concatenate([low, jnp.zeros_like(low)], axis=1),
            ],
            axis=0,
        )
        z = lax.dot_general(weights, data, NT, preferred_element_type=jnp.float32)
        z = z[: 3 * nrow] + z[3 * nrow :]
        older = h_ref[g, r : r + 1, :]
        newer = h_ref[g, 8 + r : 9 + r, :]
        first = jnp.sum(v[nrow : 2 * nrow] * newer + v[:nrow] * older, axis=1, keepdims=True)
        second = jnp.sum(v[:nrow] * newer, axis=1, keepdims=True)
        past = pltpu.roll(z[nrow : 2 * nrow], 1, 1) + pltpu.roll(z[:nrow], 2, 1)
        second = z[nrow : 2 * nrow, :1] + second
        start = jnp.where(lane == 0, first, jnp.where(lane == 1, second, past[:, :HOP]))
        total = z[2 * nrow :] + jnp.concatenate([start, past[:, HOP:]], axis=1)
        for k in range(nseg // 128):
            s_ref[i % 2, k, pl.ds(c16, nrow, stride=16), :] = total[:, k * 128 : (k + 1) * 128]
        if i > 0:
            for j in range(c16 * nrow // 16, (c16 + 1) * nrow // 16):
                finish(i - 1, j)
    for j in range(nrow):
        finish(width // 16 - 1, j)


def spectra(samples, before, taps, bins):
    width, span = samples.shape
    nseg = span // HOP
    nrow = 2 * bins.shape[0]

    def by_rows(a):
        n = a.shape[1] // HOP
        return a.reshape(width // 8, 8, n, HOP).transpose(0, 2, 1, 3).reshape(width // 8, n * 8, HOP)

    return pl.pallas_call(
        spectra_kernel,
        in_specs=[
            pl.BlockSpec(memory_space=pltpu.VMEM),
            pl.BlockSpec(memory_space=pl.ANY),
            pl.BlockSpec(memory_space=pltpu.VMEM),
        ],
        out_specs=pl.BlockSpec(memory_space=pltpu.VMEM),
        out_shape=jax.ShapeDtypeStruct((nrow // 2, width, 2 * nseg), jnp.bfloat16),
        scratch_shapes=[
            pltpu.VMEM((nrow, 4 * HOP), jnp.float32),
            pltpu.VMEM((width * 3 * nrow, HOP), jnp.float32),
            pltpu.VMEM((width // 8, nseg * 8, HOP), jnp.float32),
            pltpu.VMEM((2, nseg // 128, nrow * 16, 128), jnp.float32),
            pltpu.SemaphoreType.DMA((width // 8,)),
        ],
        compiler_params=pltpu.CompilerParams(vmem_limit_bytes=48 * 2**20),
        cost_estimate=pl.CostEstimate(
            flops=2 * 2 * 6 * nrow * width * span, bytes_accessed=width * span * 4, transcendentals=0
        ),
        name="spectra",
    )(taps_and_bins(taps, bins), by_rows(samples), by_rows(before))


def columns_of(ref, y, core):
    _, width, depth = ref.shape
    nseg = depth // 2
    take = HOP // width
    cols = ref[pl.ds((2 * y + core) * take, take)].reshape(HOP, depth)
    turned = jnp.concatenate([-cols[:, nseg:], cols[:, :nseg]], axis=1)
    return jnp.concatenate([cols, turned], axis=0)


def product(ref, r, columns):
    _, width, depth = ref.shape
    rows = ref[r : r + 4].reshape(4 * width, depth)
    return lax.dot_general(rows, columns, NT, preferred_element_type=jnp.float32)


def own_kernel(core_ref, own_hbm, p_ref, own_ref, sems):
    nsrc, width, _ = own_ref.shape
    copies = [pltpu.make_async_copy(own_hbm.at[r], own_ref.at[r], sems.at[r]) for r in range(nsrc)]
    for copy in copies:
        copy.start()
    for copy in copies:
        copy.wait()
    for y in range(p_ref.shape[0]):
        own = columns_of(own_ref, y, core_ref[0])
        for r in range(0, nsrc, 4):
            p_ref[y, r * width : (r + 4) * width, :] = product(own_ref, r, own)


def code_kernel(core_ref, other_ref, columns_ref, p_ref, o_ref):
    nsrc, width, _ = other_ref.shape
    for y in range(p_ref.shape[0]):
        other = columns_of(columns_ref, y, core_ref[0])
        for r in range(0, nsrc, 4):
            part = product(other_ref, r, other) + p_ref[y, r * width : (r + 4) * width, :]
            level = jnp.log2(jnp.maximum(jnp.abs(part), LEAST))
            code = (level * STEPS + (0.5 - math.log2(LEAST) * STEPS)).astype(jnp.int32)
            code = jnp.where(part < 0.0, -code, code).astype(jnp.int16)
            code = code.reshape(4, width, 2 * HOP)
            o_ref[y, r : r + 4, :width] = code[:, :, :HOP]
            o_ref[y, r : r + 4, width:] = code[:, :, HOP:]


def own_products(core, own, blocks):
    nsrc, width, depth = own.shape
    chans = nsrc * width
    return pl.pallas_call(
        own_kernel,
        in_specs=[
            pl.BlockSpec(memory_space=pltpu.SMEM),
            pl.BlockSpec(memory_space=pl.ANY),
        ],
        out_specs=pl.BlockSpec(memory_space=pltpu.VMEM),
        out_shape=jax.ShapeDtypeStruct((blocks, chans, 2 * HOP), jnp.float32),
        scratch_shapes=[
            pltpu.VMEM((nsrc, width, depth), jnp.bfloat16),
            pltpu.SemaphoreType.DMA((nsrc,)),
        ],
        compiler_params=pltpu.CompilerParams(vmem_limit_bytes=24 * 2**20),
        cost_estimate=pl.CostEstimate(
            flops=4 * chans * blocks * HOP * depth,
            bytes_accessed=2 * chans * (depth + 4 * blocks * HOP),
            transcendentals=0,
        ),
        name="own_products",
    )(core, own)


def product_codes(core, other, partial):
    nsrc, width, depth = other.shape
    blocks, chans, _ = partial.shape
    return pl.pallas_call(
        code_kernel,
        in_specs=[
            pl.BlockSpec(memory_space=pltpu.SMEM),
            pl.BlockSpec(memory_space=pltpu.VMEM),
            pl.BlockSpec(memory_space=pltpu.VMEM),
            pl.BlockSpec(memory_space=pltpu.VMEM),
        ],
        out_specs=pl.BlockSpec(memory_space=pltpu.VMEM),
        out_shape=jax.ShapeDtypeStruct((blocks, nsrc, 2 * width, HOP), jnp.int16),
        compiler_params=pltpu.CompilerParams(vmem_limit_bytes=32 * 2**20),
        cost_estimate=pl.CostEstimate(
            flops=4 * chans * blocks * HOP * depth,
            bytes_accessed=2 * chans * (depth + 6 * blocks * HOP),
            transcendentals=chans * blocks * HOP * 2,
        ),
        name="product_codes",
    )(core, other, other, partial)


def total_kernel(scale, c_ref, o_ref, buf, sems):
    blocks, nbin, _, _ = c_ref.shape
    width = buf.shape[2]
    copies = []
    for b in range(nbin):
        total = jnp.zeros((2 * width, HOP), jnp.float32)
        for y in range(blocks):
            code = c_ref[y, b].astype(jnp.int32).astype(jnp.float32)
            level = jnp.abs(code) * (1.0 / STEPS) + math.log2(LEAST * scale)
            size = jnp.exp2(level)
            total = total + jnp.where(code > 0.0, size, jnp.where(code < 0.0, -size, 0.0))
        buf[0, b] = total[:width]
        buf[1, b] = total[width:]
        if b % 2 == 1:
            both = pl.ds(b - 1, 2)
            copy = pltpu.make_async_copy(buf.at[:, both], o_ref.at[:, both], sems.at[b // 2])
            copy.start()
            copies.append(copy)
    for copy in copies:
        copy.wait()


def total_of(codes, scale):
    blocks, nbin, height, _ = codes.shape
    width = height // 2
    return pl.pallas_call(
        functools.partial(total_kernel, scale),
        in_specs=[pl.BlockSpec(memory_space=pltpu.VMEM)],
        out_specs=pl.BlockSpec(memory_space=pltpu.HBM),
        out_shape=jax.ShapeDtypeStruct((2, nbin, width, HOP), jnp.float32),
        scratch_shapes=[
            pltpu.VMEM((2, nbin, width, HOP), jnp.float32),
            pltpu.SemaphoreType.DMA((nbin // 2,)),
        ],
        compiler_params=pltpu.CompilerParams(vmem_limit_bytes=32 * 2**20),
        cost_estimate=pl.CostEstimate(
            flops=6 * blocks * nbin * height * HOP,
            bytes_accessed=3 * blocks * nbin * height * HOP,
            transcendentals=blocks * nbin * height * HOP,
        ),
        name="total",
    )(codes)


def body(samples, taps, bins):
    width, span = samples.shape
    times, chans = lax.axis_size("tm"), lax.axis_size("chan")
    before = passed_along(samples[:, span - SEG :], "tm", 1)
    own = spectra(samples, before, taps, bins)
    mine = lax.all_to_all(own, "chan", 0, 0)
    other = lax.ppermute(mine, "tm", [(i, i ^ 1) for i in range(times)])
    core = (lax.axis_index("tm") % 2).astype(jnp.int32).reshape(1)
    codes = product_codes(core, other, own_products(core, mine, times // 2))
    height = codes.shape[2]
    same_core = [[t * chans + c for t in range(h, times, 2) for c in range(chans)] for h in range(2)]
    codes = lax.all_to_all(
        codes.reshape(times // 2 * chans, height, HOP),
        ("tm", "chan"),
        0,
        0,
        axis_index_groups=same_core,
    )
    scale = 1.0 / (times * (span // HOP) * 3.0 * SEG / 8.0)
    return total_of(codes.reshape(times // 2, chans, height, HOP), scale)


def solution(mesh):
    return jax.shard_map(
        body,
        mesh=mesh,
        in_specs=(P("chan", "tm"), P("chan", None), P()),
        out_specs=P(None, None, "chan", "tm"),
        check_vma=False,
    )
```

```python
import functools
import math

import jax
import jax.numpy as jnp
from jax import lax
from jax.experimental import pallas as pl
from jax.experimental.pallas import tpu as pltpu
from jax.sharding import PartitionSpec as P

SEG = 256
HOP = 128
LEAST = 2.0**-64
STEPS = 312.0
NT = (((1,), (1,)), ((), ()))


def passed_along(block, axis, distance):
    devices = range(lax.axis_size(axis))
    route = [(i - distance, i) for i in devices if i - distance in devices]
    return lax.ppermute(block, axis, route)


def split(value):
    high = value.astype(jnp.bfloat16)
    return high, (value - high.astype(jnp.float32)).astype(jnp.bfloat16)


def fill_weights(t_ref, b_ref, v_ref):
    nrow, size = b_ref.shape
    nbin = nrow // 2
    ntap, width = t_ref.shape[0] - 8, t_ref.shape[1]
    index = lax.broadcasted_iota(jnp.int32, (nrow, SEG), 1)
    odd = lax.broadcasted_iota(jnp.int32, (nrow, SEG), 0) % 2
    own_bin = lax.broadcasted_iota(jnp.int32, (nrow, nbin), 0) // 2
    own_bin = own_bin == lax.broadcasted_iota(jnp.int32, (nrow, nbin), 1)
    bins = jnp.where(own_bin, t_ref[ntap : ntap + 1, :nbin], 0.0)
    bins = jnp.sum(bins, axis=1, keepdims=True).astype(jnp.int32)
    window = 0.5 - 0.5 * jnp.cos(2.0 * jnp.pi * index.astype(jnp.float32) / SEG)
    phase = 2.0 * jnp.pi * ((bins * index) & (SEG - 1)).astype(jnp.float32) / SEG
    wave = jnp.where(odd == 0, jnp.cos(phase), -jnp.sin(phase))
    b_ref[:, :HOP] = jnp.zeros((nrow, HOP), jnp.float32)
    b_ref[:, HOP : HOP + SEG] = window * wave
    b_ref[:, HOP + SEG :] = jnp.zeros((nrow, HOP), jnp.float32)
    turn = lax.broadcasted_iota(jnp.int32, (ntap, ntap), 0)
    turn = turn + lax.broadcasted_iota(jnp.int32, (ntap, ntap), 1) == ntap - 1
    turn = jnp.where(turn, 1.0, 0.0).astype(jnp.bfloat16)
    th, tl = split(t_ref[:ntap].T)
    th = jnp.dot(th, turn, preferred_element_type=jnp.float32).astype(jnp.bfloat16)
    tl = jnp.dot(tl, turn, preferred_element_type=jnp.float32).astype(jnp.bfloat16)
    lhs = jnp.concatenate([th, tl, th], axis=1)
    for row in range(nrow):
        line = jnp.broadcast_to(b_ref[row : row + 1, :], (ntap, size))
        line = pltpu.roll(line, size - ntap + 1, 1, stride=1, stride_axis=0)
        high, low = split(line[:, : 3 * HOP])
        rhs = jnp.concatenate([high, high, low], axis=0)
        out = jnp.dot(lhs, rhs, preferred_element_type=jnp.float32)
        for g in range(3):
            for i in range(width // 16):
                at = ((i * 3 + g) * nrow + row) * 16
                part = out[i * 16 : (i + 1) * 16, g * HOP : (g + 1) * HOP]
                v_ref[at : at + 16, :] = part


def taps_and_bins(taps, bins):
    width, ntap = taps.shape
    below = lax.broadcasted_iota(jnp.int32, (ntap + 8, width), 0) >= ntap
    bins = jnp.pad(bins.astype(jnp.float32), (0, width - bins.shape[0]))
    return jnp.where(below, bins[None, :], jnp.pad(taps.T, ((0, 8), (0, 0))))


def spectra_kernel(t_ref, x_ref, h_ref, o_ref, b_ref, v_ref, x_buf, s_ref, sems):
    nrow = 2 * o_ref.shape[0]
    width = o_ref.shape[1]
    nseg = o_ref.shape[2] // 2
    groups = width // 8
    copies = [
        pltpu.make_async_copy(x_ref.at[g], x_buf.at[g], sems.at[g]) for g in range(groups)
    ]
    waits = {0: copies[:1], 1: copies[1:2], 2: copies[2:4], 4: copies[4:]}
    starts = {1: copies[4:6], 2: copies[6:]}
    for copy in copies[:4]:
        copy.start()
    fill_weights(t_ref, b_ref, v_ref)
    lane = lax.broadcasted_iota(jnp.int32, (nrow, HOP), 1)

    def finish(i, j):
        for k in range(nseg // 128):
            part = s_ref[i % 2, k, j * 16 : (j + 1) * 16, :]
            at = j % 2 * nseg + k * 128
            o_ref[j // 2, i * 16 : (i + 1) * 16, at : at + 128] = part.astype(jnp.bfloat16)

    for c in range(width):
        g, r = divmod(c, 8)
        i, c16 = divmod(c, 16)
        if r == 0:
            for copy in waits.get(g, []):
                copy.wait()
            for copy in starts.get(g, []):
                copy.start()
        x = x_buf[g, pl.ds(r, nseg, stride=8), :]
        data = jnp.concatenate(split(x), axis=1)
        v = v_ref[pl.ds(i * 3 * nrow * 16 + c16, 3 * nrow, stride=16), :]
        high, low = split(v)
        weights = jnp.concatenate(
            [
                jnp.concatenate([high, high], axis=1),
                jnp.concatenate([low, jnp.zeros_like(low)], axis=1),
            ],
            axis=0,
        )
        z = lax.dot_general(weights, data, NT, preferred_element_type=jnp.float32)
        z = z[: 3 * nrow] + z[3 * nrow :]
        older = h_ref[g, r : r + 1, :]
        newer = h_ref[g, 8 + r : 9 + r, :]
        first = jnp.sum(v[nrow : 2 * nrow] * newer + v[:nrow] * older, axis=1, keepdims=True)
        second = jnp.sum(v[:nrow] * newer, axis=1, keepdims=True)
        past = pltpu.roll(z[nrow : 2 * nrow], 1, 1) + pltpu.roll(z[:nrow], 2, 1)
        second = z[nrow : 2 * nrow, :1] + second
        start = jnp.where(lane == 0, first, jnp.where(lane == 1, second, past[:, :HOP]))
        total = z[2 * nrow :] + jnp.concatenate([start, past[:, HOP:]], axis=1)
        for k in range(nseg // 128):
            s_ref[i % 2, k, pl.ds(c16, nrow, stride=16), :] = total[:, k * 128 : (k + 1) * 128]
        if i > 0:
            for j in range(c16 * nrow // 16, (c16 + 1) * nrow // 16):
                finish(i - 1, j)
    for j in range(nrow):
        finish(width // 16 - 1, j)


def spectra(samples, before, taps, bins):
    width, span = samples.shape
    nseg = span // HOP
    nrow = 2 * bins.shape[0]

    def by_rows(a):
        n = a.shape[1] // HOP
        return a.reshape(width // 8, 8, n, HOP).transpose(0, 2, 1, 3).reshape(width // 8, n * 8, HOP)

    return pl.pallas_call(
        spectra_kernel,
        in_specs=[
            pl.BlockSpec(memory_space=pltpu.VMEM),
            pl.BlockSpec(memory_space=pl.ANY),
            pl.BlockSpec(memory_space=pltpu.VMEM),
        ],
        out_specs=pl.BlockSpec(memory_space=pltpu.VMEM),
        out_shape=jax.ShapeDtypeStruct((nrow // 2, width, 2 * nseg), jnp.bfloat16),
        scratch_shapes=[
            pltpu.VMEM((nrow, 4 * HOP), jnp.float32),
            pltpu.VMEM((width * 3 * nrow, HOP), jnp.float32),
            pltpu.VMEM((width // 8, nseg * 8, HOP), jnp.float32),
            pltpu.VMEM((2, nseg // 128, nrow * 16, 128), jnp.float32),
            pltpu.SemaphoreType.DMA((width // 8,)),
        ],
        compiler_params=pltpu.CompilerParams(vmem_limit_bytes=48 * 2**20),
        cost_estimate=pl.CostEstimate(
            flops=2 * 2 * 6 * nrow * width * span, bytes_accessed=width * span * 4, transcendentals=0
        ),
        name="spectra",
    )(taps_and_bins(taps, bins), by_rows(samples), by_rows(before))


def columns_of(ref, y, core):
    _, width, depth = ref.shape
    nseg = depth // 2
    take = HOP // width
    cols = ref[pl.ds((2 * y + core) * take, take)].reshape(HOP, depth)
    turned = jnp.concatenate([-cols[:, nseg:], cols[:, :nseg]], axis=1)
    return jnp.concatenate([cols, turned], axis=0)


def product(ref, r, columns):
    _, width, depth = ref.shape
    rows = ref[r : r + 4].reshape(4 * width, depth)
    return lax.dot_general(rows, columns, NT, preferred_element_type=jnp.float32)


def own_kernel(core_ref, own_hbm, p_ref, own_ref, sems):
    nsrc, width, _ = own_ref.shape
    copies = [pltpu.make_async_copy(own_hbm.at[r], own_ref.at[r], sems.at[r]) for r in range(nsrc)]
    for copy in copies:
        copy.start()
    for copy in copies:
        copy.wait()
    for y in range(p_ref.shape[0]):
        own = columns_of(own_ref, y, core_ref[0])
        for r in range(0, nsrc, 4):
            p_ref[y, r * width : (r + 4) * width, :] = product(own_ref, r, own)


def code_kernel(core_ref, other_ref, columns_ref, p_ref, o_ref):
    nsrc, width, _ = other_ref.shape
    for y in range(p_ref.shape[0]):
        other = columns_of(columns_ref, y, core_ref[0])
        for r in range(0, nsrc, 4):
            part = product(other_ref, r, other) + p_ref[y, r * width : (r + 4) * width, :]
            level = jnp.log2(jnp.maximum(jnp.abs(part), LEAST))
            code = (level * STEPS + (0.5 - math.log2(LEAST) * STEPS)).astype(jnp.int32)
            code = jnp.where(part < 0.0, -code, code).astype(jnp.int16)
            code = code.reshape(4, width, 2 * HOP)
            o_ref[y, r : r + 4, :width] = code[:, :, :HOP]
            o_ref[y, r : r + 4, width:] = code[:, :, HOP:]


def own_products(core, own, blocks):
    nsrc, width, depth = own.shape
    chans = nsrc * width
    return pl.pallas_call(
        own_kernel,
        in_specs=[
            pl.BlockSpec(memory_space=pltpu.SMEM),
            pl.BlockSpec(memory_space=pl.ANY),
        ],
        out_specs=pl.BlockSpec(memory_space=pltpu.VMEM),
        out_shape=jax.ShapeDtypeStruct((blocks, chans, 2 * HOP), jnp.float32),
        scratch_shapes=[
            pltpu.VMEM((nsrc, width, depth), jnp.bfloat16),
            pltpu.SemaphoreType.DMA((nsrc,)),
        ],
        compiler_params=pltpu.CompilerParams(vmem_limit_bytes=24 * 2**20),
        cost_estimate=pl.CostEstimate(
            flops=4 * chans * blocks * HOP * depth,
            bytes_accessed=2 * chans * (depth + 4 * blocks * HOP),
            transcendentals=0,
        ),
        name="own_products",
    )(core, own)


def product_codes(core, other, partial):
    nsrc, width, depth = other.shape
    blocks, chans, _ = partial.shape
    return pl.pallas_call(
        code_kernel,
        in_specs=[
            pl.BlockSpec(memory_space=pltpu.SMEM),
            pl.BlockSpec(memory_space=pltpu.VMEM),
            pl.BlockSpec(memory_space=pltpu.VMEM),
            pl.BlockSpec(memory_space=pltpu.VMEM),
        ],
        out_specs=pl.BlockSpec(memory_space=pltpu.VMEM),
        out_shape=jax.ShapeDtypeStruct((blocks, nsrc, 2 * width, HOP), jnp.int16),
        compiler_params=pltpu.CompilerParams(vmem_limit_bytes=32 * 2**20),
        cost_estimate=pl.CostEstimate(
            flops=4 * chans * blocks * HOP * depth,
            bytes_accessed=2 * chans * (depth + 6 * blocks * HOP),
            transcendentals=chans * blocks * HOP * 2,
        ),
        name="product_codes",
    )(core, other, other, partial)


def total_kernel(scale, c_ref, o_ref, buf, sems):
    blocks, nbin, _, _ = c_ref.shape
    width = buf.shape[2]
    copies = []
    for b in range(nbin):
        total = jnp.zeros((2 * width, HOP), jnp.float32)
        for y in range(blocks):
            code = c_ref[y, b].astype(jnp.int32).astype(jnp.float32)
            size = jnp.exp2(jnp.abs(code) * (1.0 / STEPS))
            total = total + jnp.where(code < 0.0, 1.0 - size, size - 1.0)
        total = total * (LEAST * scale)
        buf[0, b] = total[:width]
        buf[1, b] = total[width:]
        if b % 4 == 3:
            done = pl.ds(b - 3, 4)
            copy = pltpu.make_async_copy(buf.at[:, done], o_ref.at[:, done], sems.at[b // 4])
            copy.start()
            copies.append(copy)
    for copy in copies:
        copy.wait()


def total_of(codes, scale):
    blocks, nbin, height, _ = codes.shape
    width = height // 2
    return pl.pallas_call(
        functools.partial(total_kernel, scale),
        in_specs=[pl.BlockSpec(memory_space=pltpu.VMEM)],
        out_specs=pl.BlockSpec(memory_space=pltpu.HBM),
        out_shape=jax.ShapeDtypeStruct((2, nbin, width, HOP), jnp.float32),
        scratch_shapes=[
            pltpu.VMEM((2, nbin, width, HOP), jnp.float32),
            pltpu.SemaphoreType.DMA((nbin // 4,)),
        ],
        compiler_params=pltpu.CompilerParams(vmem_limit_bytes=32 * 2**20),
        cost_estimate=pl.CostEstimate(
            flops=6 * blocks * nbin * height * HOP,
            bytes_accessed=3 * blocks * nbin * height * HOP,
            transcendentals=blocks * nbin * height * HOP,
        ),
        name="total",
    )(codes)


def body(samples, taps, bins):
    width, span = samples.shape
    times, chans = lax.axis_size("tm"), lax.axis_size("chan")
    before = passed_along(samples[:, span - SEG :], "tm", 1)
    own = spectra(samples, before, taps, bins)
    mine = lax.all_to_all(own, "chan", 0, 0)
    other = lax.ppermute(mine, "tm", [(i, i ^ 1) for i in range(times)])
    core = (lax.axis_index("tm") % 2).astype(jnp.int32).reshape(1)
    codes = product_codes(core, other, own_products(core, mine, times // 2))
    height = codes.shape[2]
    same_core = [[t * chans + c for t in range(h, times, 2) for c in range(chans)] for h in range(2)]
    codes = lax.all_to_all(
        codes.reshape(times // 2 * chans, height, HOP),
        ("tm", "chan"),
        0,
        0,
        axis_index_groups=same_core,
    )
    scale = 1.0 / (times * (span // HOP) * 3.0 * SEG / 8.0)
    return total_of(codes.reshape(times // 2, chans, height, HOP), scale)


def solution(mesh):
    return jax.shard_map(
        body,
        mesh=mesh,
        in_specs=(P("chan", "tm"), P("chan", None), P()),
        out_specs=P(None, None, "chan", "tm"),
        check_vma=False,
    )
```

```python
import functools
import math

import jax
import jax.numpy as jnp
from jax import lax
from jax.experimental import pallas as pl
from jax.experimental.pallas import tpu as pltpu
from jax.sharding import PartitionSpec as P

SEG = 256
HOP = 128
LEAST = 2.0**-64
STEPS = 312.0
NT = (((1,), (1,)), ((), ()))


def passed_along(block, axis, distance):
    devices = range(lax.axis_size(axis))
    route = [(i - distance, i) for i in devices if i - distance in devices]
    return lax.ppermute(block, axis, route)


def split(value):
    high = value.astype(jnp.bfloat16)
    return high, (value - high.astype(jnp.float32)).astype(jnp.bfloat16)


def fill_weights(t_ref, b_ref, v_ref):
    nrow, size = b_ref.shape
    nbin = nrow // 2
    ntap, width = t_ref.shape[0] - 8, t_ref.shape[1]
    index = lax.broadcasted_iota(jnp.int32, (nrow, SEG), 1)
    odd = lax.broadcasted_iota(jnp.int32, (nrow, SEG), 0) % 2
    own_bin = lax.broadcasted_iota(jnp.int32, (nrow, nbin), 0) // 2
    own_bin = own_bin == lax.broadcasted_iota(jnp.int32, (nrow, nbin), 1)
    bins = jnp.where(own_bin, t_ref[ntap : ntap + 1, :nbin], 0.0)
    bins = jnp.sum(bins, axis=1, keepdims=True).astype(jnp.int32)
    window = 0.5 - 0.5 * jnp.cos(2.0 * jnp.pi * index.astype(jnp.float32) / SEG)
    phase = 2.0 * jnp.pi * ((bins * index) & (SEG - 1)).astype(jnp.float32) / SEG
    wave = jnp.where(odd == 0, jnp.cos(phase), -jnp.sin(phase))
    b_ref[:, :HOP] = jnp.zeros((nrow, HOP), jnp.float32)
    b_ref[:, HOP : HOP + SEG] = window * wave
    b_ref[:, HOP + SEG :] = jnp.zeros((nrow, HOP), jnp.float32)
    turn = lax.broadcasted_iota(jnp.int32, (ntap, ntap), 0)
    turn = turn + lax.broadcasted_iota(jnp.int32, (ntap, ntap), 1) == ntap - 1
    turn = jnp.where(turn, 1.0, 0.0).astype(jnp.bfloat16)
    th, tl = split(t_ref[:ntap].T)
    th = jnp.dot(th, turn, preferred_element_type=jnp.float32).astype(jnp.bfloat16)
    tl = jnp.dot(tl, turn, preferred_element_type=jnp.float32).astype(jnp.bfloat16)
    lhs = jnp.concatenate([th, tl, th], axis=1)
    for row in range(nrow):
        line = jnp.broadcast_to(b_ref[row : row + 1, :], (ntap, size))
        line = pltpu.roll(line, size - ntap + 1, 1, stride=1, stride_axis=0)
        high, low = split(line[:, : 3 * HOP])
        rhs = jnp.concatenate([high, high, low], axis=0)
        out = jnp.dot(lhs, rhs, preferred_element_type=jnp.float32)
        for g in range(3):
            for i in range(width // 16):
                at = ((i * 3 + g) * nrow + row) * 16
                part = out[i * 16 : (i + 1) * 16, g * HOP : (g + 1) * HOP]
                v_ref[at : at + 16, :] = part


def taps_and_bins(taps, bins):
    width, ntap = taps.shape
    below = lax.broadcasted_iota(jnp.int32, (ntap + 8, width), 0) >= ntap
    bins = jnp.pad(bins.astype(jnp.float32), (0, width - bins.shape[0]))
    return jnp.where(below, bins[None, :], jnp.pad(taps.T, ((0, 8), (0, 0))))


def spectra_kernel(t_ref, x_ref, h_ref, o_ref, b_ref, v_ref, x_buf, s_ref, sems):
    nrow = 2 * o_ref.shape[0]
    width = o_ref.shape[1]
    nseg = o_ref.shape[2] // 2
    groups = width // 8
    copies = [
        pltpu.make_async_copy(x_ref.at[g], x_buf.at[g], sems.at[g]) for g in range(groups)
    ]
    waits = {0: copies[:1], 1: copies[1:2], 2: copies[2:4], 4: copies[4:]}
    starts = {1: copies[4:6], 2: copies[6:]}
    for copy in copies[:4]:
        copy.start()
    fill_weights(t_ref, b_ref, v_ref)
    lane = lax.broadcasted_iota(jnp.int32, (nrow, HOP), 1)

    def finish(i, j):
        for k in range(nseg // 128):
            part = s_ref[i % 2, k, j * 16 : (j + 1) * 16, :]
            at = j % 2 * nseg + k * 128
            o_ref[j // 2, i * 16 : (i + 1) * 16, at : at + 128] = part.astype(jnp.bfloat16)

    for c in range(width):
        g, r = divmod(c, 8)
        i, c16 = divmod(c, 16)
        if r == 0:
            for copy in waits.get(g, []):
                copy.wait()
            for copy in starts.get(g, []):
                copy.start()
        x = x_buf[g, pl.ds(r, nseg, stride=8), :]
        data = jnp.concatenate(split(x), axis=1)
        v = v_ref[pl.ds(i * 3 * nrow * 16 + c16, 3 * nrow, stride=16), :]
        high, low = split(v)
        weights = jnp.concatenate(
            [
                jnp.concatenate([high, high], axis=1),
                jnp.concatenate([low, jnp.zeros_like(low)], axis=1),
            ],
            axis=0,
        )
        z = lax.dot_general(weights, data, NT, preferred_element_type=jnp.float32)
        z = z[: 3 * nrow] + z[3 * nrow :]
        older = h_ref[g, r : r + 1, :]
        newer = h_ref[g, 8 + r : 9 + r, :]
        first = jnp.sum(v[nrow : 2 * nrow] * newer + v[:nrow] * older, axis=1, keepdims=True)
        second = jnp.sum(v[:nrow] * newer, axis=1, keepdims=True)
        past = pltpu.roll(z[nrow : 2 * nrow], 1, 1) + pltpu.roll(z[:nrow], 2, 1)
        second = z[nrow : 2 * nrow, :1] + second
        start = jnp.where(lane == 0, first, jnp.where(lane == 1, second, past[:, :HOP]))
        total = z[2 * nrow :] + jnp.concatenate([start, past[:, HOP:]], axis=1)
        for k in range(nseg // 128):
            s_ref[i % 2, k, pl.ds(c16, nrow, stride=16), :] = total[:, k * 128 : (k + 1) * 128]
        if i > 0:
            for j in range(c16 * nrow // 16, (c16 + 1) * nrow // 16):
                finish(i - 1, j)
    for j in range(nrow):
        finish(width // 16 - 1, j)


def spectra(samples, before, taps, bins):
    width, span = samples.shape
    nseg = span // HOP
    nrow = 2 * bins.shape[0]

    def by_rows(a):
        n = a.shape[1] // HOP
        return a.reshape(width // 8, 8, n, HOP).transpose(0, 2, 1, 3).reshape(width // 8, n * 8, HOP)

    return pl.pallas_call(
        spectra_kernel,
        in_specs=[
            pl.BlockSpec(memory_space=pltpu.VMEM),
            pl.BlockSpec(memory_space=pl.ANY),
            pl.BlockSpec(memory_space=pltpu.VMEM),
        ],
        out_specs=pl.BlockSpec(memory_space=pltpu.VMEM),
        out_shape=jax.ShapeDtypeStruct((nrow // 2, width, 2 * nseg), jnp.bfloat16),
        scratch_shapes=[
            pltpu.VMEM((nrow, 4 * HOP), jnp.float32),
            pltpu.VMEM((width * 3 * nrow, HOP), jnp.float32),
            pltpu.VMEM((width // 8, nseg * 8, HOP), jnp.float32),
            pltpu.VMEM((2, nseg // 128, nrow * 16, 128), jnp.float32),
            pltpu.SemaphoreType.DMA((width // 8,)),
        ],
        compiler_params=pltpu.CompilerParams(vmem_limit_bytes=48 * 2**20),
        cost_estimate=pl.CostEstimate(
            flops=2 * 2 * 6 * nrow * width * span, bytes_accessed=width * span * 4, transcendentals=0
        ),
        name="spectra",
    )(taps_and_bins(taps, bins), by_rows(samples), by_rows(before))


def columns_of(ref, y, core):
    _, width, depth = ref.shape
    nseg = depth // 2
    take = HOP // width
    cols = ref[pl.ds((2 * y + core) * take, take)].reshape(HOP, depth)
    turned = jnp.concatenate([-cols[:, nseg:], cols[:, :nseg]], axis=1)
    return jnp.concatenate([cols, turned], axis=0)


def product(ref, r, columns):
    _, width, depth = ref.shape
    rows = ref[r : r + 4].reshape(4 * width, depth)
    return lax.dot_general(rows, columns, NT, preferred_element_type=jnp.float32)


def reversed_bits(count):
    bits = count.bit_length() - 1
    return [sum((i >> k & 1) << (bits - 1 - k) for k in range(bits)) for i in range(count)]


def own_kernel(core_ref, own_hbm, p_ref, own_ref, sems):
    nsrc, width, _ = own_ref.shape
    copies = [pltpu.make_async_copy(own_hbm.at[r], own_ref.at[r], sems.at[r]) for r in range(nsrc)]
    for copy in copies:
        copy.start()
    for copy in copies:
        copy.wait()
    for y in range(p_ref.shape[0]):
        own = columns_of(own_ref, y, core_ref[0])
        for r in range(0, nsrc, 4):
            p_ref[y, r * width : (r + 4) * width, :] = product(own_ref, r, own)


def code_kernel(core_ref, other_ref, columns_ref, p_ref, o_ref):
    nsrc, width, _ = other_ref.shape
    place = reversed_bits(o_ref.shape[0])
    for y in range(p_ref.shape[0]):
        other = columns_of(columns_ref, y, core_ref[0])
        for r in range(0, nsrc, 4):
            part = product(other_ref, r, other) + p_ref[y, r * width : (r + 4) * width, :]
            level = jnp.log2(jnp.maximum(jnp.abs(part), LEAST))
            code = (level * STEPS + (0.5 - math.log2(LEAST) * STEPS)).astype(jnp.int32)
            code = jnp.where(part < 0.0, -code, code).astype(jnp.int16)
            code = code.reshape(4, width, 2 * HOP)
            for i in range(4):
                at = place[y * nsrc + r + i]
                o_ref[at, :width] = code[i, :, :HOP]
                o_ref[at, width:] = code[i, :, HOP:]


def own_products(core, own, blocks):
    nsrc, width, depth = own.shape
    chans = nsrc * width
    return pl.pallas_call(
        own_kernel,
        in_specs=[
            pl.BlockSpec(memory_space=pltpu.SMEM),
            pl.BlockSpec(memory_space=pl.ANY),
        ],
        out_specs=pl.BlockSpec(memory_space=pltpu.VMEM),
        out_shape=jax.ShapeDtypeStruct((blocks, chans, 2 * HOP), jnp.float32),
        scratch_shapes=[
            pltpu.VMEM((nsrc, width, depth), jnp.bfloat16),
            pltpu.SemaphoreType.DMA((nsrc,)),
        ],
        compiler_params=pltpu.CompilerParams(vmem_limit_bytes=24 * 2**20),
        cost_estimate=pl.CostEstimate(
            flops=4 * chans * blocks * HOP * depth,
            bytes_accessed=2 * chans * (depth + 4 * blocks * HOP),
            transcendentals=0,
        ),
        name="own_products",
    )(core, own)


def product_codes(core, other, partial):
    nsrc, width, depth = other.shape
    blocks, chans, _ = partial.shape
    return pl.pallas_call(
        code_kernel,
        in_specs=[
            pl.BlockSpec(memory_space=pltpu.SMEM),
            pl.BlockSpec(memory_space=pltpu.VMEM),
            pl.BlockSpec(memory_space=pltpu.VMEM),
            pl.BlockSpec(memory_space=pltpu.VMEM),
        ],
        out_specs=pl.BlockSpec(memory_space=pltpu.VMEM),
        out_shape=jax.ShapeDtypeStruct((blocks * nsrc, 2 * width, HOP), jnp.int16),
        compiler_params=pltpu.CompilerParams(vmem_limit_bytes=32 * 2**20),
        cost_estimate=pl.CostEstimate(
            flops=4 * chans * blocks * HOP * depth,
            bytes_accessed=2 * chans * (depth + 6 * blocks * HOP),
            transcendentals=chans * blocks * HOP * 2,
        ),
        name="product_codes",
    )(core, other, other, partial)


def total_kernel(scale, c_ref, o_ref, buf, sems):
    _, nbin, width, _ = buf.shape
    blocks = c_ref.shape[0] // nbin
    place = reversed_bits(blocks * nbin)
    copies = []
    for b in range(nbin):
        total = jnp.zeros((2 * width, HOP), jnp.float32)
        for y in range(blocks):
            code = c_ref[place[y * nbin + b]].astype(jnp.int32).astype(jnp.float32)
            size = jnp.exp2(jnp.abs(code) * (1.0 / STEPS))
            total = total + jnp.where(code < 0.0, 1.0 - size, size - 1.0)
        total = total * (LEAST * scale)
        buf[0, b] = total[:width]
        buf[1, b] = total[width:]
        if b % 4 == 3:
            done = pl.ds(b - 3, 4)
            copy = pltpu.make_async_copy(buf.at[:, done], o_ref.at[:, done], sems.at[b // 4])
            copy.start()
            copies.append(copy)
    for copy in copies:
        copy.wait()


def total_of(codes, nbin, scale):
    count, height, _ = codes.shape
    blocks = count // nbin
    width = height // 2
    return pl.pallas_call(
        functools.partial(total_kernel, scale),
        in_specs=[pl.BlockSpec(memory_space=pltpu.VMEM)],
        out_specs=pl.BlockSpec(memory_space=pltpu.HBM),
        out_shape=jax.ShapeDtypeStruct((2, nbin, width, HOP), jnp.float32),
        scratch_shapes=[
            pltpu.VMEM((2, nbin, width, HOP), jnp.float32),
            pltpu.SemaphoreType.DMA((nbin // 4,)),
        ],
        compiler_params=pltpu.CompilerParams(vmem_limit_bytes=32 * 2**20),
        cost_estimate=pl.CostEstimate(
            flops=6 * blocks * nbin * height * HOP,
            bytes_accessed=3 * blocks * nbin * height * HOP,
            transcendentals=blocks * nbin * height * HOP,
        ),
        name="total",
    )(codes)


def body(samples, taps, bins):
    width, span = samples.shape
    times, chans = lax.axis_size("tm"), lax.axis_size("chan")
    before = passed_along(samples[:, span - SEG :], "tm", 1)
    own = spectra(samples, before, taps, bins)
    mine = lax.all_to_all(own, "chan", 0, 0)
    other = lax.ppermute(mine, "tm", [(i, i ^ 1) for i in range(times)])
    core = (lax.axis_index("tm") % 2).astype(jnp.int32).reshape(1)
    codes = product_codes(core, other, own_products(core, mine, times // 2))
    same_core = [
        [(2 * (i // chans) + h) * chans + i % chans for i in reversed_bits(times // 2 * chans)]
        for h in range(2)
    ]
    codes = lax.all_to_all(codes, ("tm", "chan"), 0, 0, axis_index_groups=same_core)
    scale = 1.0 / (times * (span // HOP) * 3.0 * SEG / 8.0)
    return total_of(codes, chans, scale)


def solution(mesh):
    return jax.shard_map(
        body,
        mesh=mesh,
        in_specs=(P("chan", "tm"), P("chan", None), P()),
        out_specs=P(None, None, "chan", "tm"),
        check_vma=False,
    )
```

```python
import functools
import math

import jax
import jax.numpy as jnp
from jax import lax
from jax.experimental import pallas as pl
from jax.experimental.pallas import tpu as pltpu
from jax.sharding import PartitionSpec as P

SEG = 256
HOP = 128
LEAST = 2.0**-64
STEPS = 312.0
NT = (((1,), (1,)), ((), ()))


def passed_along(block, axis, distance):
    devices = range(lax.axis_size(axis))
    route = [(i - distance, i) for i in devices if i - distance in devices]
    return lax.ppermute(block, axis, route)


def split(value):
    high = value.astype(jnp.bfloat16)
    return high, (value - high.astype(jnp.float32)).astype(jnp.bfloat16)


def fill_weights(t_ref, b_ref, v_ref):
    nrow, size = b_ref.shape
    nbin = nrow // 2
    ntap, width = t_ref.shape[0] - 8, t_ref.shape[1]
    index = lax.broadcasted_iota(jnp.int32, (nrow, SEG), 1)
    odd = lax.broadcasted_iota(jnp.int32, (nrow, SEG), 0) % 2
    own_bin = lax.broadcasted_iota(jnp.int32, (nrow, nbin), 0) // 2
    own_bin = own_bin == lax.broadcasted_iota(jnp.int32, (nrow, nbin), 1)
    bins = jnp.where(own_bin, t_ref[ntap : ntap + 1, :nbin], 0.0)
    bins = jnp.sum(bins, axis=1, keepdims=True).astype(jnp.int32)
    window = 0.5 - 0.5 * jnp.cos(2.0 * jnp.pi * index.astype(jnp.float32) / SEG)
    phase = 2.0 * jnp.pi * ((bins * index) & (SEG - 1)).astype(jnp.float32) / SEG
    wave = jnp.where(odd == 0, jnp.cos(phase), -jnp.sin(phase))
    b_ref[:, :HOP] = jnp.zeros((nrow, HOP), jnp.float32)
    b_ref[:, HOP : HOP + SEG] = window * wave
    b_ref[:, HOP + SEG :] = jnp.zeros((nrow, HOP), jnp.float32)
    turn = lax.broadcasted_iota(jnp.int32, (ntap, ntap), 0)
    turn = turn + lax.broadcasted_iota(jnp.int32, (ntap, ntap), 1) == ntap - 1
    turn = jnp.where(turn, 1.0, 0.0).astype(jnp.bfloat16)
    th, tl = split(t_ref[:ntap].T)
    th = jnp.dot(th, turn, preferred_element_type=jnp.float32).astype(jnp.bfloat16)
    tl = jnp.dot(tl, turn, preferred_element_type=jnp.float32).astype(jnp.bfloat16)
    lhs = jnp.concatenate([th, tl, th], axis=1)
    for row in range(nrow):
        line = jnp.broadcast_to(b_ref[row : row + 1, :], (ntap, size))
        line = pltpu.roll(line, size - ntap + 1, 1, stride=1, stride_axis=0)
        high, low = split(line[:, : 3 * HOP])
        rhs = jnp.concatenate([high, high, low], axis=0)
        out = jnp.dot(lhs, rhs, preferred_element_type=jnp.float32)
        for g in range(3):
            for i in range(width // 16):
                at = ((i * 3 + g) * nrow + row) * 16
                part = out[i * 16 : (i + 1) * 16, g * HOP : (g + 1) * HOP]
                v_ref[at : at + 16, :] = part


def taps_and_bins(taps, bins):
    width, ntap = taps.shape
    below = lax.broadcasted_iota(jnp.int32, (ntap + 8, width), 0) >= ntap
    bins = jnp.pad(bins.astype(jnp.float32), (0, width - bins.shape[0]))
    return jnp.where(below, bins[None, :], jnp.pad(taps.T, ((0, 8), (0, 0))))


def spectra_kernel(t_ref, x_ref, h_ref, o_ref, b_ref, v_ref, x_buf, s_ref, sems):
    nrow = 2 * o_ref.shape[0]
    width = o_ref.shape[1]
    nseg = o_ref.shape[2] // 2
    groups = width // 8
    copies = [
        pltpu.make_async_copy(x_ref.at[g], x_buf.at[g], sems.at[g]) for g in range(groups)
    ]
    waits = {0: copies[:1], 1: copies[1:2], 2: copies[2:4], 4: copies[4:]}
    starts = {1: copies[4:6], 2: copies[6:]}
    for copy in copies[:4]:
        copy.start()
    fill_weights(t_ref, b_ref, v_ref)
    lane = lax.broadcasted_iota(jnp.int32, (nrow, HOP), 1)

    def finish(i, j):
        for k in range(nseg // 128):
            part = s_ref[i % 2, k, j * 16 : (j + 1) * 16, :]
            at = j % 2 * nseg + k * 128
            o_ref[j // 2, i * 16 : (i + 1) * 16, at : at + 128] = part.astype(jnp.bfloat16)

    for c in range(width):
        g, r = divmod(c, 8)
        i, c16 = divmod(c, 16)
        if r == 0:
            for copy in waits.get(g, []):
                copy.wait()
            for copy in starts.get(g, []):
                copy.start()
        x = x_buf[g, pl.ds(r, nseg, stride=8), :]
        data = jnp.concatenate(split(x), axis=1)
        v = v_ref[pl.ds(i * 3 * nrow * 16 + c16, 3 * nrow, stride=16), :]
        high, low = split(v)
        weights = jnp.concatenate(
            [
                jnp.concatenate([high, high], axis=1),
                jnp.concatenate([low, jnp.zeros_like(low)], axis=1),
            ],
            axis=0,
        )
        z = lax.dot_general(weights, data, NT, preferred_element_type=jnp.float32)
        z = z[: 3 * nrow] + z[3 * nrow :]
        older = h_ref[g, r : r + 1, :]
        newer = h_ref[g, 8 + r : 9 + r, :]
        first = jnp.sum(v[nrow : 2 * nrow] * newer + v[:nrow] * older, axis=1, keepdims=True)
        second = jnp.sum(v[:nrow] * newer, axis=1, keepdims=True)
        past = pltpu.roll(z[nrow : 2 * nrow], 1, 1) + pltpu.roll(z[:nrow], 2, 1)
        second = z[nrow : 2 * nrow, :1] + second
        start = jnp.where(lane == 0, first, jnp.where(lane == 1, second, past[:, :HOP]))
        total = z[2 * nrow :] + jnp.concatenate([start, past[:, HOP:]], axis=1)
        for k in range(nseg // 128):
            s_ref[i % 2, k, pl.ds(c16, nrow, stride=16), :] = total[:, k * 128 : (k + 1) * 128]
        if i > 0:
            for j in range(c16 * nrow // 16, (c16 + 1) * nrow // 16):
                finish(i - 1, j)
    for j in range(nrow):
        finish(width // 16 - 1, j)


def spectra(samples, before, taps, bins):
    width, span = samples.shape
    nseg = span // HOP
    nrow = 2 * bins.shape[0]

    def by_rows(a):
        n = a.shape[1] // HOP
        return a.reshape(width // 8, 8, n, HOP).transpose(0, 2, 1, 3).reshape(width // 8, n * 8, HOP)

    return pl.pallas_call(
        spectra_kernel,
        in_specs=[
            pl.BlockSpec(memory_space=pltpu.VMEM),
            pl.BlockSpec(memory_space=pl.ANY),
            pl.BlockSpec(memory_space=pltpu.VMEM),
        ],
        out_specs=pl.BlockSpec(memory_space=pltpu.VMEM),
        out_shape=jax.ShapeDtypeStruct((nrow // 2, width, 2 * nseg), jnp.bfloat16),
        scratch_shapes=[
            pltpu.VMEM((nrow, 4 * HOP), jnp.float32),
            pltpu.VMEM((width * 3 * nrow, HOP), jnp.float32),
            pltpu.VMEM((width // 8, nseg * 8, HOP), jnp.float32),
            pltpu.VMEM((2, nseg // 128, nrow * 16, 128), jnp.float32),
            pltpu.SemaphoreType.DMA((width // 8,)),
        ],
        compiler_params=pltpu.CompilerParams(vmem_limit_bytes=48 * 2**20),
        cost_estimate=pl.CostEstimate(
            flops=2 * 2 * 6 * nrow * width * span, bytes_accessed=width * span * 4, transcendentals=0
        ),
        name="spectra",
    )(taps_and_bins(taps, bins), by_rows(samples), by_rows(before))


def columns_of(ref, y, core):
    _, width, depth = ref.shape
    nseg = depth // 2
    take = HOP // width
    cols = ref[pl.ds((2 * y + core) * take, take)].reshape(HOP, depth)
    turned = jnp.concatenate([-cols[:, nseg:], cols[:, :nseg]], axis=1)
    return jnp.concatenate([cols, turned], axis=0)


def product(ref, r, columns):
    _, width, depth = ref.shape
    rows = ref[r : r + 4].reshape(4 * width, depth)
    return lax.dot_general(rows, columns, NT, preferred_element_type=jnp.float32)


def spread_order(count):
    bits = count.bit_length() - 1
    taken = [*range(bits - 1, -1, -2), *range(bits - 2, -1, -2)]
    return [sum((p >> k & 1) << taken[k] for k in range(bits)) for p in range(count)]


def places(count):
    order = spread_order(count)
    return [order.index(i) for i in range(count)]


def own_kernel(core_ref, own_hbm, p_ref, own_ref, sems):
    nsrc, width, _ = own_ref.shape
    copies = [pltpu.make_async_copy(own_hbm.at[r], own_ref.at[r], sems.at[r]) for r in range(nsrc)]
    for copy in copies:
        copy.start()
    for copy in copies:
        copy.wait()
    for y in range(p_ref.shape[0]):
        own = columns_of(own_ref, y, core_ref[0])
        for r in range(0, nsrc, 4):
            p_ref[y, r * width : (r + 4) * width, :] = product(own_ref, r, own)


def code_kernel(core_ref, other_ref, columns_ref, p_ref, o_ref):
    nsrc, width, _ = other_ref.shape
    place = places(o_ref.shape[0])
    for y in range(p_ref.shape[0]):
        other = columns_of(columns_ref, y, core_ref[0])
        for r in range(0, nsrc, 4):
            part = product(other_ref, r, other) + p_ref[y, r * width : (r + 4) * width, :]
            level = jnp.log2(jnp.maximum(jnp.abs(part), LEAST))
            code = (level * STEPS + (0.5 - math.log2(LEAST) * STEPS)).astype(jnp.int32)
            code = jnp.where(part < 0.0, -code, code).astype(jnp.int16)
            code = code.reshape(4, width, 2 * HOP)
            for i in range(4):
                at = place[y * nsrc + r + i]
                o_ref[at, :width] = code[i, :, :HOP]
                o_ref[at, width:] = code[i, :, HOP:]


def own_products(core, own, blocks):
    nsrc, width, depth = own.shape
    chans = nsrc * width
    return pl.pallas_call(
        own_kernel,
        in_specs=[
            pl.BlockSpec(memory_space=pltpu.SMEM),
            pl.BlockSpec(memory_space=pl.ANY),
        ],
        out_specs=pl.BlockSpec(memory_space=pltpu.VMEM),
        out_shape=jax.ShapeDtypeStruct((blocks, chans, 2 * HOP), jnp.float32),
        scratch_shapes=[
            pltpu.VMEM((nsrc, width, depth), jnp.bfloat16),
            pltpu.SemaphoreType.DMA((nsrc,)),
        ],
        compiler_params=pltpu.CompilerParams(vmem_limit_bytes=24 * 2**20),
        cost_estimate=pl.CostEstimate(
            flops=4 * chans * blocks * HOP * depth,
            bytes_accessed=2 * chans * (depth + 4 * blocks * HOP),
            transcendentals=0,
        ),
        name="own_products",
    )(core, own)


def product_codes(core, other, partial):
    nsrc, width, depth = other.shape
    blocks, chans, _ = partial.shape
    return pl.pallas_call(
        code_kernel,
        in_specs=[
            pl.BlockSpec(memory_space=pltpu.SMEM),
            pl.BlockSpec(memory_space=pltpu.VMEM),
            pl.BlockSpec(memory_space=pltpu.VMEM),
            pl.BlockSpec(memory_space=pltpu.VMEM),
        ],
        out_specs=pl.BlockSpec(memory_space=pltpu.VMEM),
        out_shape=jax.ShapeDtypeStruct((blocks * nsrc, 2 * width, HOP), jnp.int16),
        compiler_params=pltpu.CompilerParams(vmem_limit_bytes=32 * 2**20),
        cost_estimate=pl.CostEstimate(
            flops=4 * chans * blocks * HOP * depth,
            bytes_accessed=2 * chans * (depth + 6 * blocks * HOP),
            transcendentals=chans * blocks * HOP * 2,
        ),
        name="product_codes",
    )(core, other, other, partial)


def total_kernel(scale, c_ref, o_ref, buf, sems):
    _, nbin, width, _ = buf.shape
    blocks = c_ref.shape[0] // nbin
    place = places(blocks * nbin)
    copies = []
    for b in range(nbin):
        total = jnp.zeros((2 * width, HOP), jnp.float32)
        for y in range(blocks):
            code = c_ref[place[y * nbin + b]].astype(jnp.int32).astype(jnp.float32)
            size = jnp.exp2(jnp.abs(code) * (1.0 / STEPS))
            total = total + jnp.where(code < 0.0, 1.0 - size, size - 1.0)
        total = total * (LEAST * scale)
        buf[0, b] = total[:width]
        buf[1, b] = total[width:]
        if b % 4 == 3:
            done = pl.ds(b - 3, 4)
            copy = pltpu.make_async_copy(buf.at[:, done], o_ref.at[:, done], sems.at[b // 4])
            copy.start()
            copies.append(copy)
    for copy in copies:
        copy.wait()


def total_of(codes, nbin, scale):
    count, height, _ = codes.shape
    blocks = count // nbin
    width = height // 2
    return pl.pallas_call(
        functools.partial(total_kernel, scale),
        in_specs=[pl.BlockSpec(memory_space=pltpu.VMEM)],
        out_specs=pl.BlockSpec(memory_space=pltpu.HBM),
        out_shape=jax.ShapeDtypeStruct((2, nbin, width, HOP), jnp.float32),
        scratch_shapes=[
            pltpu.VMEM((2, nbin, width, HOP), jnp.float32),
            pltpu.SemaphoreType.DMA((nbin // 4,)),
        ],
        compiler_params=pltpu.CompilerParams(vmem_limit_bytes=32 * 2**20),
        cost_estimate=pl.CostEstimate(
            flops=6 * blocks * nbin * height * HOP,
            bytes_accessed=3 * blocks * nbin * height * HOP,
            transcendentals=blocks * nbin * height * HOP,
        ),
        name="total",
    )(codes)


def body(samples, taps, bins):
    width, span = samples.shape
    times, chans = lax.axis_size("tm"), lax.axis_size("chan")
    before = passed_along(samples[:, span - SEG :], "tm", 1)
    own = spectra(samples, before, taps, bins)
    mine = lax.all_to_all(own, "chan", 0, 0)
    other = lax.ppermute(mine, "tm", [(i, i ^ 1) for i in range(times)])
    core = (lax.axis_index("tm") % 2).astype(jnp.int32).reshape(1)
    codes = product_codes(core, other, own_products(core, mine, times // 2))
    same_core = [
        [(2 * (i // chans) + h) * chans + i % chans for i in spread_order(times // 2 * chans)]
        for h in range(2)
    ]
    codes = lax.all_to_all(codes, ("tm", "chan"), 0, 0, axis_index_groups=same_core)
    scale = 1.0 / (times * (span // HOP) * 3.0 * SEG / 8.0)
    return total_of(codes, chans, scale)


def solution(mesh):
    return jax.shard_map(
        body,
        mesh=mesh,
        in_specs=(P("chan", "tm"), P("chan", None), P()),
        out_specs=P(None, None, "chan", "tm"),
        check_vma=False,
    )
```
